32 devices in a mesh: seq: 8 (over z, y), head: 4 (over x, core).
Axes of the slice: x: 2, y: 2, z: 4, core: 2. Of those that a mesh axis runs over, the one named last changes fastest.
Arguments:
- layer_input: bfloat16 [4, 1024, 8192], P('head', 'seq'), may hold values from -6 to 6
- out_grad: bfloat16 [4, 1024, 8192], P('head', 'seq'), may hold values from -6 to 6
- attention_out: bfloat16 [4, 1024, 4096], P('head', 'seq'), may hold values from -6 to 6
- frozen_output_grad: bfloat16 [4, 1024, 4096], P('head', 'seq'), may hold values from -6 to 6
- query_rows: bfloat16 [4, 1024, 4096], P('head', 'seq'), may hold values from -120 to 120
- key_rows: bfloat16 [4, 1024, 512], P('head', 'seq'), may hold values from -4 to 4
- value_rows: bfloat16 [4, 1024, 512], P('head', 'seq'), may hold values from -6 to 6
- seg_lengths: int32 [4, 8], P('head'), may hold values from 1 to 256, 1024 in all within a row
- use_list: int32 [4, 8], replicated, may hold values from 0 to 31, as said below
- store_map: int32 [32], replicated, may hold values from 0 to 31, as said below
- query_down: float32 [32, 64, 8192], P('head', None, 'seq'), may hold values from -0.0625 to 0.0625
- query_up: float32 [32, 64, 4096], P('head', None, 'seq'), may hold values from -0.75 to 0.75
- output_down: float32 [32, 64, 4096], P('head', None, 'seq'), may hold values from -0.09375 to 0.09375
- output_up: float32 [32, 64, 8192], P('head', None, 'seq'), may hold values from -0.75 to 0.75
Outputs:
- grad_query_down: float32 [32, 64, 8192], P('head', None, 'seq')
- grad_query_up: float32 [32, 64, 4096], P('head', None, 'seq')
- grad_output_down: float32 [32, 64, 4096], P('head', None, 'seq')
- grad_output_up: float32 [32, 64, 8192], P('head', None, 'seq')
The draws below stay inside these ranges and needn't reach their ends.
Inputs may be any that keep to these rules, and one draw needn't show every extreme that they name: `use_list`: each row names 8 distinct tenants. Counting a tenant's store index as store_map[tenant] // 8, a row names at most 2 tenants of one store index, and exactly 2 of some store index in every row. A permutation: tenant t's adapters are in slot store_map[t]. `seg_lengths`: each row sums to 1024.
All inputs are finite; a program needn't handle non-finite values.
Results may differ from the reference program's by a relative error of at most 0.024.
Values may be sent and summed in bfloat16 or wider, within the bound.
A program may use at most 128 MiB of HBM per device.

```python
import math
import jax
import jax.numpy as jnp
import numpy as np
from jax import lax

D = 8192
QH = 32
KVH = 4
HD = 128
ADAPTER_RANK = 64
SLOTS_DEV = 8
ACTIVE_TENANTS = 8
CAP = 2
MB = 4
TEN = 32
SEQ_LEN = 1024
SEGMAX = 256
QD = 4096
KVD = 512


def tenant_tables(key):
    base_key = jax.random.fold_in(key, 101)
    map_key, seat_key, local_key, order_key = jax.random.split(base_key, 4)
    store_map = jax.random.permutation(map_key, TEN).astype(jnp.int32)
    slot_owner = jnp.argsort(store_map, stable=True).astype(jnp.int32)
    seat_count = MB * CAP
    seat_ids = jnp.tile(jnp.arange(seat_count, dtype=jnp.int32)[None, :], (MB, 1))
    shuffled = jax.random.permutation(seat_key, seat_ids, axis=1, independent=True)
    position = jnp.argsort(shuffled, axis=1, stable=True).astype(jnp.int32)
    first_store = shuffled[:, 0] // CAP
    seat_store = jnp.arange(seat_count, dtype=jnp.int32) // CAP
    priority = jnp.where(seat_store[None, :] == first_store[:, None], -1, position)
    chosen = jnp.argsort(priority, axis=1, stable=True)[:, :ACTIVE_TENANTS].astype(jnp.int32)
    local_table = jnp.tile(jnp.arange(SLOTS_DEV, dtype=jnp.int32)[None, :], (MB * MB, 1))
    local_table = jax.random.permutation(local_key, local_table, axis=1, independent=True).reshape(MB, MB, SLOTS_DEV)
    chosen_store = chosen // CAP
    chosen_cap = chosen % CAP
    batch_ids = jnp.arange(MB, dtype=jnp.int32)[:, None]
    local_slot = local_table[batch_ids, chosen_store, chosen_cap]
    slot_index = chosen_store * SLOTS_DEV + local_slot
    tenant = slot_owner[slot_index]
    use_list = jax.random.permutation(order_key, tenant, axis=1, independent=True)
    return (use_list.astype(jnp.int32), store_map)


def query_key_pair(key):
    base_key = jax.random.fold_in(key, 202)
    query_key, other_key = jax.random.split(base_key)
    key_draw = jnp.clip(jax.random.normal(other_key, (MB, SEQ_LEN, KVH, HD), jnp.float32), -4.0, 4.0)
    query_draw = jnp.clip(jax.random.normal(query_key, (MB, SEQ_LEN, QH, HD), jnp.float32), -4.0, 4.0)
    return (query_draw.reshape(MB, SEQ_LEN, QH * HD), key_draw.reshape(MB, SEQ_LEN, KVH * HD))


def draw_use_list(key, part):
    return tenant_tables(key)[0]


def draw_store_map(key, part):
    return tenant_tables(key)[1]


def draw_query_rows(key, part):
    return query_key_pair(key)[0].astype(jnp.bfloat16)


def draw_key_rows(key, part):
    return query_key_pair(key)[1].astype(jnp.bfloat16)


def steps_of(rng, extent, cuts, smallest, top_value):
    def one(dim, shards_of):
        steps = jax.random.uniform(jax.random.fold_in(jax.random.fold_in(rng, 6), dim), (shards_of,), jnp.float32, smallest / len(cuts), top_value / len(cuts))
        return jnp.repeat(jnp.exp(steps), extent[dim] // shards_of).reshape((-1,) + (1,) * (len(extent) - dim - 1))

    level = one(*cuts[0])
    for cut in cuts[1:]:
        level = level * one(*cut)
    return level


def length_profile(count, total, limit, slope):
    weights = [(1 << 20) // math.isqrt(grade ** slope) + 1 for grade in range(2, count + 1)]
    surplus, counts = total - limit - (count - 1), [1] * (count - 1)
    while surplus > 0:
        movable = [i for i in range(count - 1) if counts[i] < limit]
        pool, left = sum([weights[i] for i in movable]), surplus
        for i in movable:
            more = min(limit - counts[i], max(1, left * weights[i] // pool), surplus)
            counts[i] = counts[i] + more
            surplus = surplus - more
    return np.array([limit] + counts)


def uneven_parts(key, count, total, reach, skew):
    if count == 2:
        one = jax.random.randint(key, (), max(1, total - reach), min(reach, total - 1) + 1)
        return jnp.stack([one, total - one])
    sizes = jnp.asarray(length_profile(count, total, reach, skew), jnp.int32)
    pairs = (count - 1) // 2
    source_of, sink = sizes[1:1 + 2 * pairs:2], sizes[2:2 + 2 * pairs:2]
    margin = jnp.minimum(source_of - 1, reach - sink)
    passed = jax.random.randint(jax.random.fold_in(key, 1), (pairs,), 0, 1 << 20) % (margin + 1)
    sizes = sizes.at[1:1 + 2 * pairs:2].set(source_of - passed).at[2:2 + 2 * pairs:2].set(sink + passed)
    return sizes[jax.random.permutation(jax.random.fold_in(key, 2), count)]


def scatter_about(key, extent, deviation, reach, pieces=(), held_as=jnp.bfloat16):
    entries = jax.random.normal(key, extent, jnp.float32) * deviation
    if len(pieces) > 0:
        entries = steps_of(key, extent, pieces, -0.22, 0.18) * entries
    return jnp.clip(entries, min=-reach, max=reach).astype(held_as)


def setup_inputs(seed: int = 0) -> dict:
    key_list = jax.random.split(jax.random.key(seed), 15)
    layer_input = scatter_about(key_list[0], (MB, SEQ_LEN, D), 1.0, 6.0, ((0, 4), (1, 8)))
    out_grad = scatter_about(key_list[1], (MB, SEQ_LEN, D), 1.0, 6.0, ((0, 4), (1, 8)))
    attention_out = scatter_about(key_list[2], (MB, SEQ_LEN, QD), 1.0, 6.0, ((0, 4), (1, 8)))
    frozen_output_grad = scatter_about(key_list[3], (MB, SEQ_LEN, QD), 1.0, 6.0, ((0, 4), (1, 8)))
    query_rows = draw_query_rows(jax.random.fold_in(key_list[14], 71), 0)
    key_rows = draw_key_rows(jax.random.fold_in(key_list[14], 71), 0)
    value_rows = scatter_about(key_list[6], (MB, SEQ_LEN, KVD), 1.0, 6.0, ((0, 4), (1, 8)))
    seg_lengths = jax.vmap(lambda own: uneven_parts(own, ACTIVE_TENANTS, SEQ_LEN, SEGMAX, 2))(jax.random.split(key_list[7], MB)).reshape((MB, ACTIVE_TENANTS)).astype(jnp.int32)
    use_list = draw_use_list(jax.random.fold_in(key_list[14], 71), 0)
    store_map = draw_store_map(jax.random.fold_in(key_list[14], 71), 0)
    query_down = scatter_about(key_list[10], (TEN, ADAPTER_RANK, D), D ** -0.5, 0.0625, ((0, 4), (2, 8)), jnp.float32)
    query_up = scatter_about(key_list[11], (TEN, ADAPTER_RANK, QD), ADAPTER_RANK ** -0.5, 0.75, ((0, 4), (2, 8)), jnp.float32)
    output_down = scatter_about(key_list[12], (TEN, ADAPTER_RANK, QD), QD ** -0.5, 0.09375, ((0, 4), (2, 8)), jnp.float32)
    output_up = scatter_about(key_list[13], (TEN, ADAPTER_RANK, D), ADAPTER_RANK ** -0.5, 0.75, ((0, 4), (2, 8)), jnp.float32)
    return {"layer_input": layer_input, "out_grad": out_grad, "attention_out": attention_out, "frozen_output_grad": frozen_output_grad, "query_rows": query_rows, "key_rows": key_rows, "value_rows": value_rows, "seg_lengths": seg_lengths, "use_list": use_list, "store_map": store_map, "query_down": query_down, "query_up": query_up, "output_down": output_down, "output_up": output_up}


adapter_scale = 2.0
big_negative = -1e+30

def narrow(full_rows, tenant_row_mask, rank_size):
    length, used_count = tenant_row_mask.shape
    return lax.optimization_barrier(jnp.sum(full_rows.reshape(length, used_count, rank_size) * tenant_row_mask[:, :, None], axis=1))

def widened_rows(low_rows, tenant_row_mask):
    length, used_count = tenant_row_mask.shape
    spread_rows = tenant_row_mask.astype(jnp.bfloat16)[:, :, None] * low_rows[:, None, :]
    return spread_rows.reshape(length, used_count * low_rows.shape[1])

def attention_grad(query_heads, key_heads, value_heads, gradient_heads, segment, key_span):
    length, head_count, head_width = query_heads.shape
    block_rows = min(512, length)
    window = block_rows + key_span
    factor = 1.0 / math.sqrt(head_width)
    padded_keys = jnp.pad(key_heads, ((key_span, 0), (0, 0), (0, 0)))
    padded_values = jnp.pad(value_heads, ((key_span, 0), (0, 0), (0, 0)))
    padded_segment = jnp.concatenate([jnp.full((key_span,), -1, jnp.int32), segment.astype(jnp.int32)])

    def one_block(row_start):
        query_block = lax.dynamic_slice_in_dim(query_heads, row_start, block_rows, 0).astype(jnp.float32)
        grad_block = lax.dynamic_slice_in_dim(gradient_heads, row_start, block_rows, 0).astype(jnp.float32)
        key_block = lax.dynamic_slice_in_dim(padded_keys, row_start, window, 0).astype(jnp.float32)
        value_block = lax.dynamic_slice_in_dim(padded_values, row_start, window, 0).astype(jnp.float32)
        query_segment = lax.dynamic_slice_in_dim(segment, row_start, block_rows, 0)
        key_segment = lax.dynamic_slice_in_dim(padded_segment, row_start, window, 0)
        query_pos = row_start + jnp.arange(block_rows, dtype=jnp.int32)
        key_pos = row_start - key_span + jnp.arange(window, dtype=jnp.int32)
        allowed = (query_segment[:, None] == key_segment[None, :]) & (key_pos[None, :] <= query_pos[:, None])
        scores = jnp.einsum('qhd,khd->hqk', query_block, key_block) * factor
        scores = jnp.where(allowed[None, :, :], scores, big_negative)
        row_max = lax.optimization_barrier(jnp.max(scores, axis=2, keepdims=True))
        weights = jnp.exp(scores - row_max)
        probabilities = weights / lax.optimization_barrier(jnp.sum(weights, axis=2, keepdims=True))
        prob_grad = jnp.einsum('qhd,khd->hqk', grad_block, value_block)
        inner = lax.optimization_barrier(jnp.sum(probabilities * prob_grad, axis=2, keepdims=True))
        score_grad = (probabilities * (prob_grad - inner)).astype(jnp.bfloat16)
        query_gradient = jnp.einsum('hqk,khd->qhd', score_grad.astype(jnp.float32), key_block) * factor
        return query_gradient.astype(jnp.bfloat16)
    starts = jnp.arange(0, length, block_rows, dtype=jnp.int32)
    return lax.map(one_block, starts).reshape(length, head_count * head_width)

def reference(layer_input, out_grad, attention_out, frozen_output_grad, query_rows, key_rows, value_rows, seg_lengths, use_list, store_map, query_down, query_up, output_down, output_up):
    store_list = (query_down, query_up, output_down, output_up)
    adapter_gradients = [jnp.zeros(part.shape, jnp.float32) for part in store_list]
    positions = jnp.arange(SEQ_LEN, dtype=jnp.int32)
    used_ids = jnp.arange(ACTIVE_TENANTS, dtype=jnp.int32)
    group_size = QH // KVH
    for micro_batch_index in range(MB):
        tenant_slot_list = store_map[use_list[micro_batch_index]].astype(jnp.int32)
        flattened_list = [part[tenant_slot_list].astype(jnp.bfloat16).reshape(ACTIVE_TENANTS * ADAPTER_RANK, -1) for part in store_list]
        lengths = seg_lengths[micro_batch_index].astype(jnp.int32)
        offsets = (jnp.cumsum(lengths) - lengths).astype(jnp.int32)
        segment = (lax.optimization_barrier(jnp.sum((positions[:, None] >= offsets[None, :]).astype(jnp.int32), axis=1)) - 1).astype(jnp.int32)
        tenant_row_mask = (segment[:, None] == used_ids[None, :]).astype(jnp.float32)
        inputs_now = layer_input[micro_batch_index]
        grads_now = out_grad[micro_batch_index]
        outputs_now = attention_out[micro_batch_index]
        low_rank_output = narrow(jnp.dot(outputs_now, flattened_list[2].T, preferred_element_type=jnp.float32), tenant_row_mask, ADAPTER_RANK).astype(jnp.bfloat16)
        low_grad = narrow(jnp.dot(grads_now, flattened_list[3].T, preferred_element_type=jnp.float32), tenant_row_mask, ADAPTER_RANK).astype(jnp.bfloat16)
        low_rank_query = narrow(jnp.dot(inputs_now, flattened_list[0].T, preferred_element_type=jnp.float32), tenant_row_mask, ADAPTER_RANK).astype(jnp.bfloat16)
        widened_gradient = widened_rows(low_grad, tenant_row_mask)
        gradient_heads = (frozen_output_grad[micro_batch_index].astype(jnp.float32) + adapter_scale * jnp.dot(widened_gradient, flattened_list[2], preferred_element_type=jnp.float32)).astype(jnp.bfloat16)
        key_heads = jnp.repeat(key_rows[micro_batch_index].reshape(SEQ_LEN, KVH, HD), group_size, axis=1)
        value_heads = jnp.repeat(value_rows[micro_batch_index].reshape(SEQ_LEN, KVH, HD), group_size, axis=1)
        query_gradient = attention_grad(query_rows[micro_batch_index].reshape(SEQ_LEN, QH, HD), key_heads, value_heads, gradient_heads.reshape(SEQ_LEN, QH, HD), segment, SEGMAX)
        low_rank_back = narrow(jnp.dot(query_gradient, flattened_list[1].T, preferred_element_type=jnp.float32), tenant_row_mask, ADAPTER_RANK).astype(jnp.bfloat16)
        outer_products = (jnp.dot(widened_rows(low_rank_back, tenant_row_mask).T, inputs_now, preferred_element_type=jnp.float32), jnp.dot(widened_rows(low_rank_query, tenant_row_mask).T, query_gradient, preferred_element_type=jnp.float32), jnp.dot(widened_gradient.T, outputs_now, preferred_element_type=jnp.float32), jnp.dot(widened_rows(low_rank_output, tenant_row_mask).T, grads_now, preferred_element_type=jnp.float32))
        adapter_gradients = [running_total.at[tenant_slot_list].add(adapter_scale * adapter_term.reshape(ACTIVE_TENANTS, ADAPTER_RANK, -1)) for running_total, adapter_term in zip(adapter_gradients, outer_products)]
    return (adapter_gradients[0], adapter_gradients[1], adapter_gradients[2], adapter_gradients[3])
```

```python
import functools
import math

import jax
import jax.numpy as jnp
from jax import lax
from jax.experimental import pallas as pl
from jax.experimental.pallas import tpu as pltpu
from jax.sharding import PartitionSpec as P

QH = 32
KVH = 4
HD = 128
CAP = 2
LANES = 128
TILE = 256

adapter_scale = 2.0
big_negative = -1e30
MESH = pl.DeviceIdType.MESH
bf16 = jnp.bfloat16
f32 = jnp.float32


def dot(left_side, right_side, left_dim=1, right_dim=0):
    return lax.dot_general(
        left_side,
        right_side,
        (((left_dim,), (right_dim,)), ((), ())),
        preferred_element_type=f32,
    )


def gradient_kernel(
    n, groups,
    x_ref, g_ref, a_ref, f_ref, q_ref, k_ref, v_ref,
    seg_ref, use_ref, map_ref,
    qd_ref, qu_ref, od_ref, ou_ref,
    rqd_ref, rqu_ref, rod_ref, rou_ref,
    xc, gc, ac, fc, qc, kc, vc,
    sqd, squ, sod, sou,
    kqd, kqu, kod, kou,
    pqd, pqu, pod, pou,
    dqd, dqu, dod, dou,
    part, gathered, low, wide, qg,
    store_sem, tok_send, tok_recv, tok_local,
    pan_send, pan_recv, pan_local,
    rs_send, rs_recv, ag_send, ag_recv,
    ret_send, ret_recv, ret_local,
):
    me = lax.axis_index("seq")
    mine = lax.axis_index("head")
    rows = x_ref.shape[1]
    half = rows // 2
    length = n * rows
    span = length // 4
    window = TILE + span
    slots_dev, rank_size = qd_ref.shape[0], qd_ref.shape[1]
    seat_rows = groups * CAP * rank_size
    used = use_ref.shape[1]
    heads_here = QH // n
    group_size = QH // KVH
    factor = 1.0 / math.sqrt(HD)
    pairs = seat_rows // LANES
    block = CAP * rank_size

    stores = ((qd_ref, sqd), (qu_ref, squ), (od_ref, sod), (ou_ref, sou))
    for i, (source, target) in enumerate(stores):
        pltpu.make_async_copy(source, target, store_sem.at[i]).start()

    barrier = pltpu.get_barrier_semaphore()

    def greet_seq(k, carry):
        pl.semaphore_signal(
            barrier, inc=1, device_id={"seq": lax.rem(me + k, n)}, device_id_type=MESH
        )
        return carry

    def greet_head(k, carry):
        pl.semaphore_signal(
            barrier, inc=1, device_id={"head": lax.rem(mine + k, groups)}, device_id_type=MESH
        )
        return carry

    lax.fori_loop(1, n, greet_seq, 0)
    lax.fori_loop(1, groups, greet_head, 0)
    pl.semaphore_wait(barrier, n + groups - 2)

    def kv_head(p):
        return (p * heads_here) // group_size

    tokens = (
        (g_ref, gc, 0, None),
        (f_ref, fc, 0, None),
        (q_ref, qc, 0, None),
        (k_ref, kc, span, kv_head),
        (v_ref, vc, span, kv_head),
        (a_ref, ac, 0, None),
        (x_ref, xc, 0, None),
    )

    def send_tokens(i):
        source, target, first, head_of = tokens[i]
        width = target.shape[1]

        def view(p):
            column = p if head_of is None else head_of(p)
            return source.at[0, :, pl.ds(pl.multiple_of(column * width, LANES), width)]

        landing = target.at[pl.ds(pl.multiple_of(first + me * rows, rows), rows)]

        def one(k, carry):
            p = lax.rem(me + k, n)
            pltpu.make_async_remote_copy(
                src_ref=view(p), dst_ref=landing, send_sem=tok_send.at[i], recv_sem=tok_recv.at[i],
                device_id={"seq": p}, device_id_type=MESH,
            ).start()
            return carry

        lax.fori_loop(1, n, one, 0)
        pltpu.make_async_copy(view(me), landing, tok_local.at[i]).start()

    def all_bytes(ref, sem):
        pltpu.make_async_copy(ref, ref, sem).wait()

    def token_bytes(i):
        return tokens[i][1].at[pl.ds(0, (n - 1) * rows)]

    def wait_tokens(i):
        all_bytes(token_bytes(i), tok_recv.at[i])
        all_bytes(tokens[i][1].at[pl.ds(0, rows)], tok_local.at[i])

    for i in range(5):
        send_tokens(i)
    kc[pl.ds(0, span), :] = jnp.zeros((span, HD), bf16)
    vc[pl.ds(0, span), :] = jnp.zeros((span, HD), bf16)

    def slot_of(m, i):
        return map_ref[use_ref[m, i]]

    picks = []
    for m in range(groups):
        count = jnp.int32(0)
        index = [jnp.int32(0)] * CAP
        for i in range(used):
            slot = slot_of(m, i)
            hit = (slot // slots_dev) == mine
            for c in range(CAP):
                index[c] = jnp.where(hit & (count == c), slot % slots_dev, index[c])
            count = count + jnp.where(hit, 1, 0)
        picks.append((index, count))

    panels = ((sqd, kqd, pqd), (squ, kqu, pqu), (sod, kod, pod), (sou, kou, pou))

    def send_panels(i):
        store, packed, target = panels[i]
        pltpu.make_async_copy(stores[i][0], store, store_sem.at[i]).wait()
        for m in range(groups):
            index, count = picks[m]
            for c in range(CAP):
                panel = store[index[c]]
                keep = jnp.where(count > c, 1.0, 0.0).astype(f32)
                packed[pl.ds(m * block + c * rank_size, rank_size), :] = (panel * keep).astype(bf16)
        landing = target.at[pl.ds(pl.multiple_of(mine * block, block), block)]

        def one(k, carry):
            p = lax.rem(mine + k, groups)
            pltpu.make_async_remote_copy(
                src_ref=packed.at[pl.ds(pl.multiple_of(p * block, block), block)],
                dst_ref=landing, send_sem=pan_send.at[i], recv_sem=pan_recv.at[i],
                device_id={"head": p}, device_id_type=MESH,
            ).start()
            return carry

        lax.fori_loop(1, groups, one, 0)
        pltpu.make_async_copy(
            packed.at[pl.ds(pl.multiple_of(mine * block, block), block)], landing, pan_local.at[i]
        ).start()

    def wait_panels(i):
        target = panels[i][2]
        all_bytes(target.at[pl.ds(0, (groups - 1) * block)], pan_recv.at[i])
        all_bytes(target.at[pl.ds(0, block)], pan_local.at[i])

    for i in (3, 2, 1, 0):
        send_panels(i)

    owners = [slot_of(mine, i) // slots_dev for i in range(used)]
    seats, offsets, total = [], [], jnp.int32(0)
    for i in range(used):
        rank = jnp.int32(0)
        for j in range(i):
            rank = rank + jnp.where(owners[j] == owners[i], 1, 0)
        seats.append(owners[i] * CAP + rank)
        offsets.append(total)
        total = total + seg_ref[0, i]

    def chosen(positions, values):
        result = jnp.full(positions.shape, values[0], jnp.int32)
        for i in range(1, used):
            result = jnp.where(positions >= offsets[i], values[i], result)
        return result

    def column_positions(tile):
        return tile * TILE + lax.broadcasted_iota(jnp.int32, (TILE, 1), 0)

    upper = (lax.broadcasted_iota(jnp.int32, (1, LANES), 1) >= rank_size).astype(jnp.int32)
    upper_row = (lax.broadcasted_iota(jnp.int32, (LANES, 1), 0) >= rank_size).astype(jnp.int32)

    def at(start, size):
        return pl.ds(pl.multiple_of(start, size), size)

    def narrow(full_rows, seat):
        kept = full_rows[:, :LANES]
        pair = seat // 2
        for q in range(1, pairs):
            kept = jnp.where(pair == q, full_rows[:, q * LANES:(q + 1) * LANES], kept)
        turned = pltpu.roll(kept, rank_size, 1)
        return jnp.where((seat % 2) == upper, kept, turned)

    def pack_rows(twice):
        pieces = []
        for start in range(0, TILE, rows):
            pieces.append(
                jnp.where(upper == 0, twice[start:start + half], twice[start + half:start + rows])
            )
        return jnp.concatenate(pieces, axis=0)

    def unpack_rows(packed):
        packed = packed.astype(f32)
        turned = pltpu.roll(packed, rank_size, 1)
        first = jnp.where(upper == 0, packed, turned)
        second = jnp.where(upper == 0, turned, packed)
        pieces = []
        for start in range(0, TILE // 2, half):
            pieces += [first[start:start + half], second[start:start + half]]
        return jnp.concatenate(pieces, axis=0)

    def project(e, columns, panel):
        def one(tile, carry):
            seat = chosen(column_positions(tile), seats)
            full_rows = dot(columns[at(tile * TILE, TILE), :], panel[...], 1, 1)
            part[e, at(tile * (TILE // 2), TILE // 2), :] = pack_rows(
                narrow(full_rows, seat)
            ).astype(bf16)
            return carry

        lax.fori_loop(0, length // TILE, one, 0)

    def start_sum(e):
        def one(k, carry):
            p = lax.rem(me + k, n)
            pltpu.make_async_remote_copy(
                src_ref=part.at[e, at(p * half, half)], dst_ref=gathered.at[e, me],
                send_sem=rs_send.at[e], recv_sem=rs_recv.at[e],
                device_id={"seq": p}, device_id_type=MESH,
            ).start()
            return carry

        lax.fori_loop(1, n, one, 0)

    def share_sum(e):
        all_bytes(gathered.at[e, pl.ds(0, n - 1)], rs_recv.at[e])

        def add(k, running):
            return running + gathered[e, lax.rem(me + k, n)].astype(f32)

        summed = lax.fori_loop(1, n, add, part[e, at(me * half, half), :].astype(f32))
        low[e, at(me * half, half), :] = summed.astype(bf16)

        def one(k, carry):
            own = low.at[e, at(me * half, half)]
            pltpu.make_async_remote_copy(
                src_ref=own, dst_ref=own, send_sem=ag_send.at[e], recv_sem=ag_recv.at[e],
                device_id={"seq": lax.rem(me + k, n)}, device_id_type=MESH,
            ).start()
            return carry

        lax.fori_loop(1, n, one, 0)

    def low_bytes(e):
        return low.at[e, pl.ds(0, (n - 1) * half)]

    def wait_sum(e):
        all_bytes(low_bytes(e), ag_recv.at[e])

    def low_tile(e, tile):
        return unpack_rows(low[e, at(tile * (TILE // 2), TILE // 2), :])

    def widen_across(e):
        def one(tile, carry):
            low_turned = low_tile(e, tile).T
            positions = tile * TILE + lax.broadcasted_iota(jnp.int32, (1, TILE), 1)
            seat = chosen(positions, seats)
            for q in range(pairs):
                wide[pl.ds(q * LANES, LANES), at(tile * TILE, TILE)] = jnp.where(
                    seat == 2 * q + upper_row, low_turned, 0.0
                ).astype(bf16)
            return carry

        lax.fori_loop(0, length // TILE, one, 0)

    returns = ((dqd, rqd_ref), (dqu, rqu_ref), (dod, rod_ref), (dou, rou_ref))

    def outer(i, columns):
        target, landing = returns[i]
        step = min(TILE, target.shape[1])

        def one(c, carry):
            target[:, at(c * step, step)] = (
                adapter_scale * dot(wide[...], columns[:, at(c * step, step)])
            ).astype(bf16)
            return carry

        lax.fori_loop(0, target.shape[1] // step, one, 0)

        def send(k, carry):
            p = lax.rem(mine + k, groups)
            pltpu.make_async_remote_copy(
                src_ref=target.at[at(p * block, block)], dst_ref=landing.at[mine],
                send_sem=ret_send.at[i], recv_sem=ret_recv.at[i],
                device_id={"head": p}, device_id_type=MESH,
            ).start()
            return carry

        lax.fori_loop(1, groups, send, 0)
        pltpu.make_async_copy(
            target.at[at(mine * block, block)], landing.at[mine], ret_local.at[i]
        ).start()

    wait_panels(3)
    wait_tokens(0)
    project(0, gc, pou)
    start_sum(0)
    send_tokens(5)
    share_sum(0)
    wait_panels(2)
    wait_panels(1)
    wait_sum(0)
    for i in range(1, 5):
        wait_tokens(i)
    send_tokens(6)

    def attend(tile, carry):
        here = at(tile * TILE, TILE)
        positions = column_positions(tile)
        seat = chosen(positions, seats)
        start = chosen(positions, offsets)
        low_rows = low_tile(0, tile)
        widened = jnp.concatenate(
            [jnp.where(seat == 2 * q + upper, low_rows, 0.0).astype(bf16) for q in range(pairs)],
            axis=1,
        )
        heads_grad = (
            fc[here, :].astype(f32) + adapter_scale * dot(widened, pod[...])
        ).astype(bf16)
        keys = kc[pl.ds(pl.multiple_of(tile * TILE, TILE), window), :]
        values = vc[pl.ds(pl.multiple_of(tile * TILE, TILE), window), :]
        key_pos = tile * TILE - span + lax.broadcasted_iota(jnp.int32, (1, window), 1)
        allowed = (key_pos >= start) & (key_pos <= positions)
        for h in range(heads_here):
            lanes = slice(h * HD, (h + 1) * HD)
            scores = dot(qc[here, lanes], keys, 1, 1) * factor
            scores = jnp.where(allowed, scores, big_negative)
            weights = jnp.exp(scores - jnp.max(scores, axis=1, keepdims=True))
            weights = weights * (1.0 / jnp.sum(weights, axis=1, keepdims=True))
            prob_grad = dot(heads_grad[:, lanes], values, 1, 1)
            inner = jnp.sum(weights * prob_grad, axis=1, keepdims=True)
            score_grad = (weights * (prob_grad - inner)).astype(bf16)
            qg[here, lanes] = (dot(score_grad, keys) * factor).astype(bf16)
        full_rows = dot(qg[here, :], pqu[...], 1, 1)
        part[1, at(tile * (TILE // 2), TILE // 2), :] = pack_rows(
            narrow(full_rows, seat)
        ).astype(bf16)
        return carry

    lax.fori_loop(0, length // TILE, attend, 0)
    start_sum(1)

    wait_tokens(5)
    project(2, ac, pod)
    start_sum(2)
    widen_across(0)
    outer(2, ac)
    share_sum(1)
    share_sum(2)
    wait_sum(2)
    widen_across(2)
    outer(3, gc)
    wait_panels(0)
    wait_sum(1)
    wait_tokens(6)
    project(3, xc, pqd)
    start_sum(3)
    widen_across(1)
    outer(0, xc)
    share_sum(3)
    wait_sum(3)
    widen_across(3)
    outer(1, qg)

    for i in range(7):
        all_bytes(token_bytes(i), tok_send.at[i])
    for i in range(4):
        all_bytes(panels[i][2].at[pl.ds(0, (groups - 1) * block)], pan_send.at[i])
        all_bytes(gathered.at[i, pl.ds(0, n - 1)], rs_send.at[i])
        all_bytes(low_bytes(i), ag_send.at[i])
    for i in (2, 3, 0, 1):
        landing = returns[i][1]
        all_bytes(landing.at[pl.ds(0, groups - 1)], ret_recv.at[i])
        all_bytes(landing.at[0], ret_local.at[i])
        all_bytes(landing.at[pl.ds(0, groups - 1)], ret_send.at[i])


def settle_kernel(slots_dev, rank_size, use_ref, map_ref, *refs):
    groups, used = use_ref.shape
    slot = lax.axis_index("head") * slots_dev + pl.program_id(0)
    owner = lax.axis_index("head")
    found, places = [], []
    for m in range(groups):
        count, place, hit_any = jnp.int32(0), jnp.int32(0), jnp.int32(0)
        for i in range(used):
            other = map_ref[use_ref[m, i]]
            hit = other == slot
            place = jnp.where(hit, count, place)
            hit_any = jnp.where(hit, 1, hit_any)
            count = count + jnp.where(other // slots_dev == owner, 1, 0)
        found.append(hit_any.astype(f32))
        places.append(place)
    for source, target in zip(refs[:4], refs[4:]):
        total = jnp.zeros((rank_size, target.shape[2]), f32)
        for m in range(groups):
            rows = pl.ds(pl.multiple_of(places[m] * rank_size, rank_size), rank_size)
            total = total + source[m, rows, :].astype(f32) * found[m]
        target[0] = total


def shards(mesh, *arguments):
    layer_input, _, attention_out = arguments[:3]
    n, groups = mesh.shape["seq"], mesh.shape["head"]
    stores = arguments[10:]
    slots_dev, rank_size = stores[0].shape[:2]
    use_list, store_map = arguments[8], arguments[9]
    rows = layer_input.shape[1]
    length = n * rows
    wide_columns, narrow_columns = layer_input.shape[2] // n, attention_out.shape[2] // n
    block = CAP * rank_size
    span = length // 4
    widths = [store.shape[2] for store in stores]
    vmem = pltpu.VMEM
    dma = pltpu.SemaphoreType.DMA
    anywhere = pl.BlockSpec(memory_space=pl.ANY)
    scalars = pl.BlockSpec(memory_space=pltpu.SMEM)
    scratch = [
        vmem((length, wide_columns), bf16),
        vmem((length, wide_columns), bf16),
        vmem((length, narrow_columns), bf16),
        vmem((length, narrow_columns), bf16),
        vmem((length, narrow_columns), bf16),
        vmem((span + length, HD), bf16),
        vmem((span + length, HD), bf16),
    ]
    scratch += [vmem(store.shape, f32) for store in stores]
    for _ in range(3):
        scratch += [vmem((groups * block, width), bf16) for width in widths]
    scratch += [
        vmem((4, length // 2, LANES), bf16),
        vmem((4, n, rows // 2, LANES), bf16),
        vmem((4, length // 2, LANES), bf16),
        vmem((groups * block, length), bf16),
        vmem((length, narrow_columns), bf16),
        dma((4,)), dma((7,)), dma((7,)), dma((7,)),
        dma((4,)), dma((4,)), dma((4,)),
        dma((4,)), dma((4,)), dma((4,)), dma((4,)),
        dma((4,)), dma((4,)), dma((4,)),
    ]
    returned = pl.pallas_call(
        functools.partial(gradient_kernel, n, groups),
        out_shape=[jax.ShapeDtypeStruct((groups, block, width), bf16) for width in widths],
        in_specs=[anywhere] * 7 + [scalars] * 3 + [anywhere] * 4,
        out_specs=[anywhere] * 4,
        scratch_shapes=scratch,
        compiler_params=pltpu.CompilerParams(
            collective_id=0, has_side_effects=True, vmem_limit_bytes=60 * 1024 * 1024
        ),
        cost_estimate=pl.CostEstimate(
            flops=12_000_000_000, bytes_accessed=24_000_000, transcendentals=2_000_000
        ),
        name="adapter_backward",
    )(*arguments)
    return tuple(
        pl.pallas_call(
            functools.partial(settle_kernel, slots_dev, rank_size),
            grid=(slots_dev,),
            out_shape=[jax.ShapeDtypeStruct(store.shape, f32) for store in stores],
            in_specs=[scalars] * 2 + [pl.BlockSpec(memory_space=pltpu.VMEM)] * 4,
            out_specs=[
                pl.BlockSpec((1, rank_size, width), lambda s: (s, 0, 0)) for width in widths
            ],
            compiler_params=pltpu.CompilerParams(vmem_limit_bytes=32 * 1024 * 1024),
            name="settle_slots",
        )(use_list, store_map, *returned)
    )


def solution(mesh):
    token_rows = P("head", "seq", None)
    store = P("head", None, "seq")
    return jax.shard_map(
        functools.partial(shards, mesh),
        mesh=mesh,
        in_specs=(token_rows,) * 7 + (P("head", None), P(), P()) + (store,) * 4,
        out_specs=(store,) * 4,
        check_vma=False,
    )
```

```python
import functools
import math

import jax
import jax.numpy as jnp
from jax import lax
from jax.experimental import pallas as pl
from jax.experimental.pallas import tpu as pltpu
from jax.sharding import PartitionSpec as P

QH = 32
KVH = 4
HD = 128
CAP = 2
LANES = 128
TILE = 256

adapter_scale = 2.0
big_negative = -1e30
MESH = pl.DeviceIdType.MESH
bf16 = jnp.bfloat16
f32 = jnp.float32


def dot(left_side, right_side, left_dim=1, right_dim=0):
    return lax.dot_general(
        left_side,
        right_side,
        (((left_dim,), (right_dim,)), ((), ())),
        preferred_element_type=f32,
    )


def gradient_kernel(
    n, groups,
    x_ref, g_ref, a_ref, f_ref, q_ref, k_ref, v_ref,
    seg_ref, use_ref, map_ref,
    qd_ref, qu_ref, od_ref, ou_ref,
    rqd_ref, rqu_ref, rod_ref, rou_ref,
    xc, gc, ac, fc, qc, kc, vc,
    sqd, squ, sod, sou,
    kqd, kqu, kod, kou,
    pqd, pqu, pod, pou,
    dqd, dqu, dod, dou,
    part, gathered, low, wide, qg,
    store_sem, tok_send, tok_recv, tok_local,
    pan_send, pan_recv, pan_local,
    rs_send, rs_recv, ag_send, ag_recv,
    ret_send, ret_recv, ret_local,
):
    me = lax.axis_index("seq")
    mine = lax.axis_index("head")
    rows = x_ref.shape[1]
    half = rows // 2
    length = n * rows
    span = length // 4
    window = TILE + span
    slots_dev, rank_size = qd_ref.shape[0], qd_ref.shape[1]
    seat_rows = groups * CAP * rank_size
    used = use_ref.shape[1]
    heads_here = QH // n
    group_size = QH // KVH
    factor = 1.0 / math.sqrt(HD)
    pairs = seat_rows // LANES
    block = CAP * rank_size

    stores = ((qd_ref, sqd), (qu_ref, squ), (od_ref, sod), (ou_ref, sou))
    for i, (source, target) in enumerate(stores):
        pltpu.make_async_copy(source, target, store_sem.at[i]).start()

    barrier = pltpu.get_barrier_semaphore()

    def greet_seq(k, carry):
        pl.semaphore_signal(
            barrier, inc=1, device_id={"seq": lax.rem(me + k, n)}, device_id_type=MESH
        )
        return carry

    def greet_head(k, carry):
        pl.semaphore_signal(
            barrier, inc=1, device_id={"head": lax.rem(mine + k, groups)}, device_id_type=MESH
        )
        return carry

    lax.fori_loop(1, n, greet_seq, 0)
    lax.fori_loop(1, groups, greet_head, 0)
    pl.semaphore_wait(barrier, n + groups - 2)

    def kv_head(p):
        return (p * heads_here) // group_size

    tokens = (
        (g_ref, gc, 0, None),
        (f_ref, fc, 0, None),
        (q_ref, qc, 0, None),
        (k_ref, kc, span, kv_head),
        (v_ref, vc, span, kv_head),
        (a_ref, ac, 0, None),
        (x_ref, xc, 0, None),
    )

    def send_tokens(i, piece=0, pieces=1):
        source, target, first, head_of = tokens[i]
        width = target.shape[1]
        count = rows // pieces

        def view(p):
            column = p if head_of is None else head_of(p)
            return source.at[
                0, pl.ds(piece * count, count), pl.ds(pl.multiple_of(column * width, LANES), width)
            ]

        landing = target.at[pl.ds(pl.multiple_of(first + me * rows + piece * count, count), count)]

        def one(k, carry):
            p = lax.rem(me + k, n)
            pltpu.make_async_remote_copy(
                src_ref=view(p), dst_ref=landing, send_sem=tok_send.at[i], recv_sem=tok_recv.at[i],
                device_id={"seq": p}, device_id_type=MESH,
            ).start()
            return carry

        lax.fori_loop(1, n, one, 0)
        pltpu.make_async_copy(view(me), landing, tok_local.at[i]).start()

    def all_bytes(ref, sem):
        pltpu.make_async_copy(ref, ref, sem).wait()

    def token_bytes(i):
        return tokens[i][1].at[pl.ds(0, (n - 1) * rows)]

    def wait_tokens(i):
        all_bytes(token_bytes(i), tok_recv.at[i])
        all_bytes(tokens[i][1].at[pl.ds(0, rows)], tok_local.at[i])

    send_tokens(0)
    send_tokens(1)
    kc[pl.ds(0, span), :] = jnp.zeros((span, HD), bf16)
    vc[pl.ds(0, span), :] = jnp.zeros((span, HD), bf16)

    def slot_of(m, i):
        return map_ref[use_ref[m, i]]

    picks = []
    for m in range(groups):
        count = jnp.int32(0)
        index = [jnp.int32(0)] * CAP
        for i in range(used):
            slot = slot_of(m, i)
            hit = (slot // slots_dev) == mine
            for c in range(CAP):
                index[c] = jnp.where(hit & (count == c), slot % slots_dev, index[c])
            count = count + jnp.where(hit, 1, 0)
        picks.append((index, count))

    panels = ((sqd, kqd, pqd), (squ, kqu, pqu), (sod, kod, pod), (sou, kou, pou))

    def send_panels(i):
        store, packed, target = panels[i]
        pltpu.make_async_copy(stores[i][0], store, store_sem.at[i]).wait()
        for m in range(groups):
            index, count = picks[m]
            for c in range(CAP):
                panel = store[index[c]]
                keep = jnp.where(count > c, 1.0, 0.0).astype(f32)
                packed[pl.ds(m * block + c * rank_size, rank_size), :] = (panel * keep).astype(bf16)
        landing = target.at[pl.ds(pl.multiple_of(mine * block, block), block)]

        def one(k, carry):
            p = lax.rem(mine + k, groups)
            pltpu.make_async_remote_copy(
                src_ref=packed.at[pl.ds(pl.multiple_of(p * block, block), block)],
                dst_ref=landing, send_sem=pan_send.at[i], recv_sem=pan_recv.at[i],
                device_id={"head": p}, device_id_type=MESH,
            ).start()
            return carry

        lax.fori_loop(1, groups, one, 0)
        pltpu.make_async_copy(
            packed.at[pl.ds(pl.multiple_of(mine * block, block), block)], landing, pan_local.at[i]
        ).start()

    def wait_panels(i):
        target = panels[i][2]
        all_bytes(target.at[pl.ds(0, (groups - 1) * block)], pan_recv.at[i])
        all_bytes(target.at[pl.ds(0, block)], pan_local.at[i])

    for i in (3, 2, 1, 0):
        send_panels(i)

    owners = [slot_of(mine, i) // slots_dev for i in range(used)]
    seats, offsets, total = [], [], jnp.int32(0)
    for i in range(used):
        rank = jnp.int32(0)
        for j in range(i):
            rank = rank + jnp.where(owners[j] == owners[i], 1, 0)
        seats.append(owners[i] * CAP + rank)
        offsets.append(total)
        total = total + seg_ref[0, i]

    def chosen(positions, values):
        result = jnp.full(positions.shape, values[0], jnp.int32)
        for i in range(1, used):
            result = jnp.where(positions >= offsets[i], values[i], result)
        return result

    def column_positions(tile):
        return tile * TILE + lax.broadcasted_iota(jnp.int32, (TILE, 1), 0)

    upper = (lax.broadcasted_iota(jnp.int32, (1, LANES), 1) >= rank_size).astype(jnp.int32)
    upper_row = (lax.broadcasted_iota(jnp.int32, (LANES, 1), 0) >= rank_size).astype(jnp.int32)

    def at(start, size):
        return pl.ds(pl.multiple_of(start, size), size)

    def narrow(full_rows, seat):
        kept = full_rows[:, :LANES]
        pair = seat // 2
        for q in range(1, pairs):
            kept = jnp.where(pair == q, full_rows[:, q * LANES:(q + 1) * LANES], kept)
        turned = pltpu.roll(kept, rank_size, 1)
        return jnp.where((seat % 2) == upper, kept, turned)

    def pack_rows(twice):
        pieces = []
        for start in range(0, TILE, rows):
            pieces.append(
                jnp.where(upper == 0, twice[start:start + half], twice[start + half:start + rows])
            )
        return jnp.concatenate(pieces, axis=0)

    def unpack_rows(packed):
        packed = packed.astype(f32)
        turned = pltpu.roll(packed, rank_size, 1)
        first = jnp.where(upper == 0, packed, turned)
        second = jnp.where(upper == 0, turned, packed)
        pieces = []
        for start in range(0, TILE // 2, half):
            pieces += [first[start:start + half], second[start:start + half]]
        return jnp.concatenate(pieces, axis=0)

    def project(e, columns, panel):
        def one(tile, carry):
            seat = chosen(column_positions(tile), seats)
            full_rows = dot(columns[at(tile * TILE, TILE), :], panel[...], 1, 1)
            part[e, at(tile * (TILE // 2), TILE // 2), :] = pack_rows(
                narrow(full_rows, seat)
            ).astype(bf16)
            return carry

        lax.fori_loop(0, length // TILE, one, 0)

    def start_sum(e):
        def one(k, carry):
            p = lax.rem(me + k, n)
            pltpu.make_async_remote_copy(
                src_ref=part.at[e, at(p * half, half)], dst_ref=gathered.at[e, me],
                send_sem=rs_send.at[e], recv_sem=rs_recv.at[e],
                device_id={"seq": p}, device_id_type=MESH,
            ).start()
            return carry

        lax.fori_loop(1, n, one, 0)

    def share_sum(e):
        all_bytes(gathered.at[e, pl.ds(0, n - 1)], rs_recv.at[e])

        def add(k, running):
            return running + gathered[e, lax.rem(me + k, n)].astype(f32)

        summed = lax.fori_loop(1, n, add, part[e, at(me * half, half), :].astype(f32))
        low[e, at(me * half, half), :] = summed.astype(bf16)

        def one(k, carry):
            own = low.at[e, at(me * half, half)]
            pltpu.make_async_remote_copy(
                src_ref=own, dst_ref=own, send_sem=ag_send.at[e], recv_sem=ag_recv.at[e],
                device_id={"seq": lax.rem(me + k, n)}, device_id_type=MESH,
            ).start()
            return carry

        lax.fori_loop(1, n, one, 0)

    def low_bytes(e):
        return low.at[e, pl.ds(0, (n - 1) * half)]

    def wait_sum(e):
        all_bytes(low_bytes(e), ag_recv.at[e])

    def low_tile(e, tile):
        return unpack_rows(low[e, at(tile * (TILE // 2), TILE // 2), :])

    def widen_across(e, slot=0):
        def one(tile, carry):
            low_turned = low_tile(e, tile).T
            positions = tile * TILE + lax.broadcasted_iota(jnp.int32, (1, TILE), 1)
            seat = chosen(positions, seats)
            for q in range(pairs):
                wide[slot, pl.ds(q * LANES, LANES), at(tile * TILE, TILE)] = jnp.where(
                    seat == 2 * q + upper_row, low_turned, 0.0
                ).astype(bf16)
            return carry

        lax.fori_loop(0, length // TILE, one, 0)

    returns = ((dqd, rqd_ref), (dqu, rqu_ref), (dod, rod_ref), (dou, rou_ref))

    def outer(i, columns, slot=0):
        target, landing = returns[i]
        step = min(TILE, target.shape[1])

        def one(c, carry):
            target[:, at(c * step, step)] = (
                adapter_scale * dot(wide[slot], columns[:, at(c * step, step)])
            ).astype(bf16)
            return carry

        lax.fori_loop(0, target.shape[1] // step, one, 0)

        def send(k, carry):
            p = lax.rem(mine + k, groups)
            pltpu.make_async_remote_copy(
                src_ref=target.at[at(p * block, block)], dst_ref=landing.at[mine],
                send_sem=ret_send.at[i], recv_sem=ret_recv.at[i],
                device_id={"head": p}, device_id_type=MESH,
            ).start()
            return carry

        lax.fori_loop(1, groups, send, 0)
        pltpu.make_async_copy(
            target.at[at(mine * block, block)], landing.at[mine], ret_local.at[i]
        ).start()

    wait_panels(3)
    wait_tokens(0)
    project(0, gc, pou)
    start_sum(0)
    for i in (2, 3, 4):
        send_tokens(i)
    share_sum(0)
    send_tokens(5)
    wait_panels(2)
    wait_panels(1)
    for i in range(1, 5):
        wait_tokens(i)
    wait_sum(0)
    send_tokens(6, 0, 4)
    send_tokens(6, 1, 4)

    def attend(tile, carry):
        here = at(tile * TILE, TILE)
        positions = column_positions(tile)
        seat = chosen(positions, seats)
        start = chosen(positions, offsets)
        low_rows = low_tile(0, tile)
        widened = jnp.concatenate(
            [jnp.where(seat == 2 * q + upper, low_rows, 0.0).astype(bf16) for q in range(pairs)],
            axis=1,
        )
        heads_grad = (
            fc[here, :].astype(f32) + adapter_scale * dot(widened, pod[...])
        ).astype(bf16)
        keys = kc[pl.ds(pl.multiple_of(tile * TILE, TILE), window), :]
        values = vc[pl.ds(pl.multiple_of(tile * TILE, TILE), window), :]
        key_pos = tile * TILE - span + lax.broadcasted_iota(jnp.int32, (1, window), 1)
        allowed = (key_pos >= start) & (key_pos <= positions)
        for h in range(heads_here):
            lanes = slice(h * HD, (h + 1) * HD)
            scores = dot(qc[here, lanes], keys, 1, 1) * factor
            scores = jnp.where(allowed, scores, big_negative)
            weights = jnp.exp(scores - jnp.max(scores, axis=1, keepdims=True))
            weights = weights * (1.0 / jnp.sum(weights, axis=1, keepdims=True))
            prob_grad = dot(heads_grad[:, lanes], values, 1, 1)
            inner = jnp.sum(weights * prob_grad, axis=1, keepdims=True)
            score_grad = (weights * (prob_grad - inner)).astype(bf16)
            qg[here, lanes] = (dot(score_grad, keys) * factor).astype(bf16)
        full_rows = dot(qg[here, :], pqu[...], 1, 1)
        part[1, at(tile * (TILE // 2), TILE // 2), :] = pack_rows(
            narrow(full_rows, seat)
        ).astype(bf16)
        return carry

    lax.fori_loop(0, length // TILE, attend, 0)
    start_sum(1)
    wait_tokens(5)
    project(2, ac, pod)
    start_sum(2)
    send_tokens(6, 2, 4)
    widen_across(0)
    outer(2, ac)
    share_sum(1)
    share_sum(2)
    send_tokens(6, 3, 4)
    wait_sum(2)
    widen_across(2)
    outer(3, gc)
    wait_sum(1)
    widen_across(1, 1)
    wait_panels(0)
    wait_tokens(6)
    project(3, xc, pqd)
    start_sum(3)
    outer(0, xc, 1)
    share_sum(3)
    wait_sum(3)
    widen_across(3)
    outer(1, qg)

    for i in range(7):
        all_bytes(token_bytes(i), tok_send.at[i])
    for i in range(4):
        all_bytes(panels[i][2].at[pl.ds(0, (groups - 1) * block)], pan_send.at[i])
        all_bytes(gathered.at[i, pl.ds(0, n - 1)], rs_send.at[i])
        all_bytes(low_bytes(i), ag_send.at[i])
    for i in (2, 3, 0, 1):
        landing = returns[i][1]
        all_bytes(landing.at[pl.ds(0, groups - 1)], ret_recv.at[i])
        all_bytes(landing.at[0], ret_local.at[i])
        all_bytes(landing.at[pl.ds(0, groups - 1)], ret_send.at[i])


def settle_kernel(slots_dev, rank_size, use_ref, map_ref, *refs):
    groups, used = use_ref.shape
    owner = lax.axis_index("head")
    for target in refs[4:]:
        target[...] = jnp.zeros(target.shape, f32)

    def add_batch(m, carry):
        count = jnp.int32(0)
        for i in range(used):
            slot = map_ref[use_ref[m, i]]
            hit = slot // slots_dev == owner

            @pl.when(hit)
            def _(slot=slot, count=count):
                rows = pl.ds(pl.multiple_of(count * rank_size, rank_size), rank_size)
                for source, target in zip(refs[:4], refs[4:]):
                    target[slot % slots_dev] += source[m, rows, :].astype(f32)

            count = count + jnp.where(hit, 1, 0)
        return carry

    lax.fori_loop(0, groups, add_batch, 0)


def shards(mesh, *arguments):
    layer_input, _, attention_out = arguments[:3]
    n, groups = mesh.shape["seq"], mesh.shape["head"]
    stores = arguments[10:]
    slots_dev, rank_size = stores[0].shape[:2]
    use_list, store_map = arguments[8], arguments[9]
    rows = layer_input.shape[1]
    length = n * rows
    wide_columns, narrow_columns = layer_input.shape[2] // n, attention_out.shape[2] // n
    block = CAP * rank_size
    span = length // 4
    widths = [store.shape[2] for store in stores]
    pieces = max(1, min(widths) // LANES)
    vmem = pltpu.VMEM
    dma = pltpu.SemaphoreType.DMA
    anywhere = pl.BlockSpec(memory_space=pl.ANY)
    scalars = pl.BlockSpec(memory_space=pltpu.SMEM)
    scratch = [
        vmem((length, wide_columns), bf16),
        vmem((length, wide_columns), bf16),
        vmem((length, narrow_columns), bf16),
        vmem((length, narrow_columns), bf16),
        vmem((length, narrow_columns), bf16),
        vmem((span + length, HD), bf16),
        vmem((span + length, HD), bf16),
    ]
    scratch += [vmem(store.shape, f32) for store in stores]
    for _ in range(3):
        scratch += [vmem((groups * block, width), bf16) for width in widths]
    scratch += [
        vmem((4, length // 2, LANES), bf16),
        vmem((4, n, rows // 2, LANES), bf16),
        vmem((4, length // 2, LANES), bf16),
        vmem((2, groups * block, length), bf16),
        vmem((length, narrow_columns), bf16),
        dma((4,)), dma((7,)), dma((7,)), dma((7,)),
        dma((4,)), dma((4,)), dma((4,)),
        dma((4,)), dma((4,)), dma((4,)), dma((4,)),
        dma((4,)), dma((4,)), dma((4,)),
    ]
    returned = pl.pallas_call(
        functools.partial(gradient_kernel, n, groups),
        out_shape=[jax.ShapeDtypeStruct((groups, block, width), bf16) for width in widths],
        in_specs=[anywhere] * 7 + [scalars] * 3 + [anywhere] * 4,
        out_specs=[anywhere] * 4,
        scratch_shapes=scratch,
        compiler_params=pltpu.CompilerParams(
            collective_id=0, has_side_effects=True, vmem_limit_bytes=60 * 1024 * 1024
        ),
        cost_estimate=pl.CostEstimate(
            flops=12_000_000_000, bytes_accessed=24_000_000, transcendentals=2_000_000
        ),
        name="adapter_backward",
    )(*arguments)
    return tuple(
        pl.pallas_call(
            functools.partial(settle_kernel, slots_dev, rank_size),
            grid=(pieces,),
            out_shape=[jax.ShapeDtypeStruct(store.shape, f32) for store in stores],
            in_specs=[scalars] * 2
            + [pl.BlockSpec((groups, block, width // pieces), lambda s: (0, 0, s)) for width in widths],
            out_specs=[
                pl.BlockSpec((slots_dev, rank_size, width // pieces), lambda s: (0, 0, s))
                for width in widths
            ],
            compiler_params=pltpu.CompilerParams(vmem_limit_bytes=32 * 1024 * 1024),
            name="settle_slots",
        )(use_list, store_map, *returned)
    )


def solution(mesh):
    token_rows = P("head", "seq", None)
    store = P("head", None, "seq")
    return jax.shard_map(
        functools.partial(shards, mesh),
        mesh=mesh,
        in_specs=(token_rows,) * 7 + (P("head", None), P(), P()) + (store,) * 4,
        out_specs=(store,) * 4,
        check_vma=False,
    )
```
